256 devices in a mesh: group: 8 (over y, core), expert: 32 (over x, z).
Axes of the slice: x: 4, y: 4, z: 8, core: 2. Of those that a mesh axis runs over, the one named last changes fastest.
Arguments:
- tokens: bfloat16 [5120, 3584], P(('group', 'expert')), may hold values from -6 to 6
- expert_ids: int32 [5120, 8], P(('group', 'expert')), may hold values from 0 to 127, all different within a row; in each aligned block of 20 rows (0 to 19, 20 to 39, ...) at most 2 rows name the same one
- route_weights: float32 [5120, 8], P(('group', 'expert')), may hold values from 0.1 to 1
- w_gate: bfloat16 [8, 32, 3584, 512], P('group', 'expert'), may hold values from -0.09375 to 0.09375
- w_up: bfloat16 [8, 32, 3584, 512], P('group', 'expert'), may hold values from -0.09375 to 0.09375
- w_down: bfloat16 [8, 32, 512, 3584], P('group', 'expert'), may hold values from -0.1875 to 0.1875
Outputs:
- mixed: bfloat16 [5120, 3584], P(('group', 'expert'))
The draws below stay inside these ranges and needn't reach their ends.
Inputs may be any that keep to these rules, and one draw needn't show every extreme that they name: `expert_ids`: each row names 8 different experts. Within the tokens of one device (aligned blocks of 20 rows) no expert is named by more than 2 rows, a bound that some block reaches.
All inputs are finite; a program needn't handle non-finite values.
Results may differ from the reference program's by a relative error of at most 0.0065.
Values may be sent and summed in bfloat16 or wider, within the bound.
No kernel may reach another device: no remote copies, remote signals or barrier semaphores. Data moves between devices by JAX's collectives and lax.ppermute only.
A program may use at most 64 MiB of HBM per device.

```python
import math
import jax
import jax.numpy as jnp
import numpy as np
from jax import lax

D = 3584
HALF = 512
TOP = 8
TOK_DEV = 20
MEMBERS = 32
EXPERTS = 128
CAP = 2
TOKENS = 5120
N_GROUP = 8
N_EXPERT = 32


def level_of(key, dims, shards, least, top_value):
    def one(dim, blocks):
        draws = jax.random.uniform(jax.random.fold_in(jax.random.fold_in(key, 6), dim), (blocks,), jnp.float32, least / len(shards), top_value / len(shards))
        return jnp.repeat(jnp.exp(draws), dims[dim] // blocks).reshape((-1,) + (1,) * (len(dims) - dim - 1))

    gain = one(*shards[0])
    for cut in shards[1:]:
        gain = gain * one(*cut)
    return gain


def shared_out(rng, own, number, rows, number_of, top, most, lean):
    ranking = jax.random.permutation(rng, number_of)
    packed, common = portions_of(number_of, rows * top, most, lean, True), portions_of(number_of, rows * top, most, lean, False)
    places = jnp.arange(number_of)

    def named(lengths, rotation):
        used = int((lengths > 0).sum())
        fixed = max(1, used // 4)
        shifted = fixed + (places - fixed + rotation * (used - fixed)) % max(1, number_of - fixed)
        return jnp.zeros((number_of,), jnp.int32).at[ranking[jnp.where(places < fixed, places, shifted)]].set(jnp.asarray(lengths, jnp.int32))

    lengths = jnp.where(number % 4 == 0, named(packed, number // 4), named(common, number - number // 4 - 1))
    mixed = jax.random.permutation(jax.random.fold_in(own, 3), number_of)
    source_of, sink = mixed[0:number_of // 2 * 2:2], mixed[1:number_of // 2 * 2:2]
    slack = jnp.minimum(lengths[source_of] - 1, most - lengths[sink]) // 2
    slack = jnp.where((source_of == ranking[0]) | (sink == ranking[0]) | (lengths[sink] == 0), 0, jnp.maximum(slack, 0))
    shifted = jax.random.randint(jax.random.fold_in(own, 4), (number_of // 2,), 0, 1 << 20) % (slack + 1)
    lengths = lengths.at[source_of].add(-shifted).at[sink].add(shifted)
    items = jnp.searchsorted(jnp.cumsum(lengths), jnp.arange(rows * top), side="right").astype(jnp.int32)
    listing = items.reshape(top, rows).T
    listing = listing[jax.random.permutation(jax.random.fold_in(own, 1), rows)]
    rotation = jax.random.randint(jax.random.fold_in(own, 2), (rows, 1), 0, top)
    return jnp.take_along_axis(listing, (jnp.arange(top)[None, :] + rotation) % top, axis=1)


def portions_of(count, total, bound, skew, full):
    loads = [(1 << 20) // math.isqrt(standing ** skew) + 1 for standing in range(1, count + 1)]
    largest = bound if full else min(bound, max(-(-total // count), total * loads[0] // sum(loads)))
    least = 1 if total - largest >= count - 1 else 0
    counts, surplus = [largest] + [least] * (count - 1), total - largest - least * (count - 1)
    while surplus > 0:
        candidates = [i for i in range(1, count) if counts[i] < largest] or [i for i in range(1, count) if counts[i] < bound]
        whole, left = sum([loads[i] for i in candidates]), surplus
        for i in candidates:
            more = min(bound - counts[i], max(1, left * loads[i] // whole), surplus)
            counts[i] = counts[i] + more
            surplus = surplus - more
    return np.array(counts)


def scatter_about(own_key, dims, spread, reach, cuts=(), kind=jnp.bfloat16):
    gain = level_of(own_key, dims, cuts, -0.22, 0.18) if cuts else 1.0
    array = jax.random.normal(own_key, dims, jnp.float32) * spread * gain
    return jnp.minimum(jnp.maximum(array, -reach), reach).astype(kind)


def setup_inputs(seed: int = 0) -> dict:
    key_list = jax.random.split(jax.random.key(seed), 7)
    tokens = scatter_about(key_list[0], (TOKENS, D), 1.0, 6.0, ((0, 256),))
    expert_ids_keys = jax.random.split(jax.random.fold_in(key_list[1], 1), TOKENS // TOK_DEV)
    expert_ids_turns = jax.random.permutation(jax.random.fold_in(key_list[1], 3), TOKENS // TOK_DEV)
    expert_ids = jax.vmap(lambda own, number: shared_out(jax.random.fold_in(key_list[1], 2), own, number, TOK_DEV, EXPERTS, TOP, CAP, 2))(expert_ids_keys, expert_ids_turns).reshape((TOKENS, TOP))
    route_weights = jnp.clip(jnp.exp(math.log(1.0) - 2.3025851 * jax.random.uniform(key_list[2], (TOKENS, TOP), jnp.float32) ** level_of(key_list[2], (TOKENS, TOP), ((0, 256),), -0.2, 0.2)), 0.1, 1.0)
    w_gate = scatter_about(key_list[3], (N_GROUP, N_EXPERT, D, HALF), D ** -0.5, 0.09375, ((0, 8), (1, 32)))
    w_up = scatter_about(key_list[4], (N_GROUP, N_EXPERT, D, HALF), D ** -0.5, 0.09375, ((0, 8), (1, 32)))
    w_down = scatter_about(key_list[5], (N_GROUP, N_EXPERT, HALF, D), (2 * HALF) ** -0.5, 0.1875, ((0, 8), (1, 32)))
    return dict(tokens=tokens, expert_ids=expert_ids, route_weights=route_weights, w_gate=w_gate, w_up=w_up, w_down=w_down)


def reference(tokens, expert_ids, route_weights, w_gate, w_up, w_down):
    devices = N_GROUP * N_EXPERT
    per_block = TOK_DEV * TOP
    block_ids = expert_ids.reshape(devices, per_block)
    one_hot = (block_ids[:, :, None] == jnp.arange(EXPERTS, dtype=jnp.int32)[None, None, :]).astype(jnp.int32)
    before = jnp.cumsum(one_hot, axis=1) - one_hot
    slot_index = jnp.sum(before * one_hot, axis=2).astype(jnp.int32)
    position = (jnp.arange(devices, dtype=jnp.int32)[:, None] * CAP + slot_index).reshape(-1)
    token_index = (jnp.arange(TOKENS * TOP, dtype=jnp.int32) // TOP).astype(jnp.int32)
    flat_ids = expert_ids.reshape(-1).astype(jnp.int32)
    row_table = jnp.zeros((EXPERTS, devices * CAP), jnp.int32).at[flat_ids, position].set(token_index)
    weight_table = jnp.zeros((EXPERTS, devices * CAP), jnp.float32).at[flat_ids, position].set(route_weights.reshape(-1))

    def add_expert(running, expert):
        pair_index = (expert // MEMBERS).astype(jnp.int32)
        member = (expert % MEMBERS).astype(jnp.int32)
        row_block = tokens[row_table[expert]]
        gate_cols = jnp.concatenate([w_gate[2 * pair_index, member], w_gate[2 * pair_index + 1, member]], axis=1)
        up_cols = jnp.concatenate([w_up[2 * pair_index, member], w_up[2 * pair_index + 1, member]], axis=1)
        gate_act = jnp.dot(row_block, gate_cols, preferred_element_type=jnp.float32)
        up_act = jnp.dot(row_block, up_cols, preferred_element_type=jnp.float32)
        hidden = (jax.nn.silu(gate_act) * up_act).astype(jnp.bfloat16)
        first_part = jnp.dot(hidden[:, :HALF], w_down[2 * pair_index, member], preferred_element_type=jnp.float32).astype(jnp.bfloat16)
        second_part = jnp.dot(hidden[:, HALF:], w_down[2 * pair_index + 1, member], preferred_element_type=jnp.float32).astype(jnp.bfloat16)
        first_part, second_part = lax.optimization_barrier((first_part, second_part))
        expert_out = (first_part.astype(jnp.float32) + second_part.astype(jnp.float32)).astype(jnp.bfloat16)
        expert_out = lax.optimization_barrier(expert_out)
        contrib = weight_table[expert][:, None] * expert_out.astype(jnp.float32)
        return running.at[row_table[expert]].add(contrib), None

    total, unused = lax.scan(add_expert, jnp.zeros((TOKENS, D), jnp.float32), jnp.arange(EXPERTS, dtype=jnp.int32))
    return total.astype(jnp.bfloat16)
```

```python
import functools

import jax
import jax.numpy as jnp
from jax import lax
from jax.experimental import pallas as pl
from jax.experimental.pallas import tpu as pltpu
from jax.sharding import Mesh, PartitionSpec as P

F32, BF16 = jnp.float32, jnp.bfloat16
SLOTS = 2
AXES = ("y", "core", "x", "z")


def slot_parts(ids, experts):
    tokens, top = ids.shape
    lane = lax.broadcasted_iota(jnp.int32, (tokens, experts * SLOTS), 1)
    named = [ids[:, k : k + 1] == lane // SLOTS for k in range(top)]
    hits = functools.reduce(jnp.logical_or, named)
    before = lax.broadcasted_iota(jnp.int32, (tokens, tokens), 1) < lax.broadcasted_iota(jnp.int32, (tokens, tokens), 0)
    rank = jnp.dot(before.astype(F32), hits.astype(F32), preferred_element_type=F32)
    here = rank == (lane % SLOTS).astype(F32)
    return named, hits & here, here


def pick_kernel(ids_ref, tokens_ref, out_ref):
    experts = out_ref.shape[0]
    unused, chosen, also_unused = slot_parts(ids_ref[...], experts)
    rows = lax.dot_general(
        chosen.astype(F32).astype(BF16), tokens_ref[...], (((0,), (0,)), ((), ())), preferred_element_type=F32
    )
    out_ref[...] = rows.astype(BF16).reshape(out_ref.shape)


def mix_kernel(ids_ref, weights_ref, rows_ref, out_ref):
    tokens = ids_ref.shape[0]
    experts, slots, features = rows_ref.shape
    named, unused, here = slot_parts(ids_ref[...], experts)
    weights = weights_ref[...]
    table = jnp.zeros(here.shape, F32)
    for k, hit in enumerate(named):
        table = table + jnp.where(hit & here, weights[:, k : k + 1], 0.0)
    high = table.astype(BF16)
    rest = table - high.astype(F32)
    mid = rest.astype(BF16)
    low = (rest - mid.astype(F32)).astype(BF16)
    rows = rows_ref[...].reshape(experts * slots, features)
    total = jnp.dot(high, rows, preferred_element_type=F32)
    total += jnp.dot(mid, rows, preferred_element_type=F32)
    total += jnp.dot(low, rows, preferred_element_type=F32)
    out_ref[...] = total.astype(BF16)


def expert_kernel(steps, mine_ref, peer_ref, gate_ref, up_ref, down_ref, mine_out, peer_out, gate_acc, up_acc, hidden):
    step = pl.program_id(0)
    half = gate_acc.shape[0] // 2

    @pl.when(step == 0)
    def _():
        gate_acc[...] = jnp.zeros_like(gate_acc)
        up_acc[...] = jnp.zeros_like(up_acc)

    @pl.when(step < steps)
    def _():
        for at, ref in ((0, mine_ref), (half, peer_ref)):
            rows = ref[...].reshape(half, ref.shape[2])
            gate_acc[at : at + half] += jnp.dot(rows, gate_ref[...], preferred_element_type=F32)
            up_acc[at : at + half] += jnp.dot(rows, up_ref[...], preferred_element_type=F32)

    @pl.when(step == steps)
    def _():
        gate = gate_acc[...]
        hidden[...] = (gate / (1.0 + jnp.exp(-gate)) * up_acc[...]).astype(BF16)

    @pl.when(step >= steps)
    def _():
        for at, ref in ((0, mine_out), (half, peer_out)):
            part = jnp.dot(hidden[at : at + half], down_ref[...], preferred_element_type=F32)
            ref[...] = part.astype(BF16).reshape(ref.shape)


def run_expert(mine, peer, gate, up, down):
    experts, slots, features = mine.shape
    units = gate.shape[1]
    steps = 4
    wide = features // steps
    first = lambda i: jnp.minimum(i, steps - 1)
    second = lambda i: jnp.maximum(i - steps, 0)
    rows_spec = pl.BlockSpec((experts, slots, wide), lambda i: (0, 0, first(i)))
    out_spec = pl.BlockSpec((experts, slots, wide), lambda i: (0, 0, second(i)))
    rows = experts * slots * 2
    return pl.pallas_call(
        functools.partial(expert_kernel, steps),
        grid=(2 * steps,),
        in_specs=[
            rows_spec,
            rows_spec,
            pl.BlockSpec((wide, units), lambda i: (first(i), 0)),
            pl.BlockSpec((wide, units), lambda i: (first(i), 0)),
            pl.BlockSpec((units, wide), lambda i: (0, second(i))),
        ],
        out_specs=[out_spec, out_spec],
        out_shape=[jax.ShapeDtypeStruct(mine.shape, BF16)] * 2,
        scratch_shapes=[
            pltpu.VMEM((rows, units), F32),
            pltpu.VMEM((rows, units), F32),
            pltpu.VMEM((rows, units), BF16),
        ],
        compiler_params=pltpu.CompilerParams(vmem_limit_bytes=40 << 20),
        cost_estimate=pl.CostEstimate(flops=6 * rows * features * units, bytes_accessed=20 << 20, transcendentals=rows * units),
    )(mine, peer, gate, up, down)


def on_device(tokens, expert_ids, route_weights, w_gate, w_up, w_down):
    features = tokens.shape[1]
    experts = lax.axis_size("y") * lax.axis_size("x") * lax.axis_size("z")
    swap = [(0, 1), (1, 0)]
    outgoing = pl.pallas_call(
        pick_kernel, out_shape=jax.ShapeDtypeStruct((experts, SLOTS, features), BF16),
        compiler_params=pltpu.CompilerParams(vmem_limit_bytes=40 << 20),
    )(expert_ids, tokens)
    mine = lax.all_to_all(outgoing, ("y", "x", "z"), 0, 0, tiled=True)
    peer = lax.ppermute(mine, "core", swap)
    mine_part, peer_part = run_expert(mine, peer, w_gate[0, 0], w_up[0, 0], w_down[0, 0])
    other_part = lax.ppermute(peer_part, "core", swap)
    total = (mine_part.astype(F32) + other_part.astype(F32)).astype(BF16)
    returned = lax.all_to_all(total, ("y", "x", "z"), 0, 0, tiled=True)
    return pl.pallas_call(
        mix_kernel, out_shape=jax.ShapeDtypeStruct(tokens.shape, BF16),
        compiler_params=pltpu.CompilerParams(vmem_limit_bytes=40 << 20),
    )(expert_ids, route_weights, returned)


def solution(mesh):
    groups, members = mesh.devices.shape
    fine = Mesh(mesh.devices.reshape(groups // 2, 2, 4, members // 4), AXES)
    rows = P(AXES, None)
    weights = P(("y", "core"), ("x", "z"), None, None)
    return jax.shard_map(
        on_device, mesh=fine, in_specs=(rows, rows, rows, weights, weights, weights), out_specs=rows, check_vma=False
    )
```

```python
import functools

import jax
import jax.numpy as jnp
from jax import lax
from jax.experimental import pallas as pl
from jax.experimental.pallas import tpu as pltpu
from jax.sharding import Mesh, PartitionSpec as P

F32, BF16 = jnp.float32, jnp.bfloat16
SLOTS = 2
AXES = ("y", "core", "x", "z")
PLANE = ("x", "y")
EXTRA = 128


def params(mib):
    return pltpu.CompilerParams(vmem_limit_bytes=mib << 20)


def pack_kernel(tokens_ref, ids_ref, weights_ref, out_ref):
    features = tokens_ref.shape[1]
    top = ids_ref.shape[1]
    weights = weights_ref[...]
    high = weights.astype(BF16)
    rest = weights - high.astype(F32)
    mid = rest.astype(BF16)
    low = (rest - mid.astype(F32)).astype(BF16)
    column = lax.broadcasted_iota(jnp.int32, (top, EXTRA), 1)
    row = lax.broadcasted_iota(jnp.int32, (top, EXTRA), 0)
    extra = jnp.zeros((tokens_ref.shape[0], EXTRA), F32)
    for place, piece in enumerate((ids_ref[...].astype(F32).astype(BF16), high, mid, low)):
        spread = (column == row + place * top).astype(F32).astype(BF16)
        extra += jnp.dot(piece, spread, preferred_element_type=F32)
    out_ref[:, :features] = tokens_ref[...]
    out_ref[:, features:] = extra.astype(BF16)


def slot_parts(extra, z, top, chips):
    tokens = extra.shape[0]
    lane = lax.broadcasted_iota(jnp.int32, (tokens, chips * SLOTS), 1)
    chip = lane // SLOTS
    expert = ((chip % 4) * 32 + (chip // 4) * 8 + z).astype(F32)
    named = [extra[:, k : k + 1] == expert for k in range(top)]
    hits = functools.reduce(jnp.logical_or, named)
    before = lax.broadcasted_iota(jnp.int32, (tokens, tokens), 1) < lax.broadcasted_iota(jnp.int32, (tokens, tokens), 0)
    rank = jnp.dot(before.astype(F32), hits.astype(F32), preferred_element_type=F32)
    here = rank == (lane % SLOTS).astype(F32)
    return named, hits, here


def pick_kernel(top, count, z_ref, *refs):
    blocks, out_ref = refs[:count], refs[-1]
    chips, unused, slots, features = out_ref.shape
    for b, block in enumerate(blocks):
        unused, hits, here = slot_parts(block[:, features:].astype(F32), z_ref[0], top, chips)
        chosen = (hits & here).astype(F32).astype(BF16)
        rows = lax.dot_general(chosen, block[:, :features], (((0,), (0,)), ((), ())), preferred_element_type=F32)
        out_ref[:, b] = rows.astype(BF16).reshape(chips, slots, features)


def pick(z, blocks, chips, top, after=()):
    features = blocks[0].shape[1] - EXTRA
    vmem = pl.BlockSpec(memory_space=pltpu.VMEM)
    return pl.pallas_call(
        functools.partial(pick_kernel, top, len(blocks)),
        in_specs=[pl.BlockSpec(memory_space=pltpu.SMEM)] + [vmem] * len(blocks) + [pl.BlockSpec(memory_space=pl.ANY)] * len(after),
        out_shape=jax.ShapeDtypeStruct((chips, len(blocks), SLOTS, features), BF16),
        compiler_params=params(16),
    )(z, *blocks, *after)


def block_mix(z, block, rows, top):
    chips, slots, features = rows.shape
    extra = block[:, features:].astype(F32)
    named, unused, here = slot_parts(extra, z, top, chips)
    rows = rows.reshape(chips * slots, features)
    total = jnp.zeros((extra.shape[0], features), F32)
    for part in (1, 2, 3):
        table = jnp.zeros(here.shape, F32)
        for k, hit in enumerate(named):
            at = part * top + k
            table = table + jnp.where(hit & here, extra[:, at : at + 1], 0.0)
        total += jnp.dot(table.astype(BF16), rows, preferred_element_type=F32)
    return total


def far_mix_kernel(top, z_ref, *refs):
    count = (len(refs) - 1) // 2
    blocks, rows_ref, outs = refs[:count], refs[count], refs[count + 1 :]
    for b in range(count):
        outs[b][...] = block_mix(z_ref[0], blocks[b], rows_ref[:, b], top).astype(BF16)


def far_mix(z, blocks, rows, top):
    vmem = pl.BlockSpec(memory_space=pltpu.VMEM)
    out = jax.ShapeDtypeStruct((blocks[0].shape[0], rows.shape[-1]), BF16)
    return pl.pallas_call(
        functools.partial(far_mix_kernel, top),
        in_specs=[pl.BlockSpec(memory_space=pltpu.SMEM)] + [vmem] * (len(blocks) + 1),
        out_shape=[out] * len(blocks),
        compiler_params=params(16),
    )(z, *blocks, rows)


def near_mix_kernel(top, z_ref, own, left1, right1, left2, right2, rows_ref, add_left, add_right, add_far, out0, out1, out2, out3, out4):
    z = z_ref[0]
    out3[...] = (block_mix(z, left2, rows_ref[:, 3], top) + add_left[...].astype(F32) + add_far[...].astype(F32)).astype(BF16)
    out4[...] = (block_mix(z, right2, rows_ref[:, 4], top) + add_right[...].astype(F32)).astype(BF16)
    out1[...] = block_mix(z, left1, rows_ref[:, 1], top).astype(BF16)
    out2[...] = block_mix(z, right1, rows_ref[:, 2], top).astype(BF16)
    out0[...] = block_mix(z, own, rows_ref[:, 0], top)


def near_mix(z, blocks, rows, adds, top):
    vmem = pl.BlockSpec(memory_space=pltpu.VMEM)
    shape = (blocks[0].shape[0], rows.shape[-1])
    return pl.pallas_call(
        functools.partial(near_mix_kernel, top),
        in_specs=[pl.BlockSpec(memory_space=pltpu.SMEM)] + [vmem] * (len(blocks) + 4),
        out_shape=[jax.ShapeDtypeStruct(shape, F32)] + [jax.ShapeDtypeStruct(shape, BF16)] * 4,
        compiler_params=params(16),
    )(z, *blocks, rows, *adds)


def join_kernel(mine_ref, other_ref, *refs):
    refs[-1][...] = (mine_ref[...].astype(F32) + other_ref[...].astype(F32)).astype(BF16)


def join(mine, other, after=()):
    vmem = pl.BlockSpec(memory_space=pltpu.VMEM)
    return pl.pallas_call(
        join_kernel,
        in_specs=[vmem] * 2 + [pl.BlockSpec(memory_space=pl.ANY)] * len(after),
        out_shape=jax.ShapeDtypeStruct(mine.shape, BF16),
        compiler_params=params(16),
    )(mine, other, *after)


def sum_kernel(own, *refs):
    total = own[...]
    for ref in refs[:-1]:
        total = total + ref[...].astype(F32)
    refs[-1][...] = total.astype(BF16)


def expert_kernel(mine_ref, peer_ref, gate_ref, up_ref, down_ref, mine_out, peer_out, rows, hidden):
    half = rows.shape[0] // 2
    features = rows.shape[1]
    units = hidden.shape[1]
    rows[:half] = mine_ref[...].reshape(half, features)
    rows[half:] = peer_ref[...].reshape(half, features)
    wide = 256

    def first(n, carry):
        cols = pl.ds(pl.multiple_of(n * wide, wide), wide)
        gate = jnp.dot(rows[...], gate_ref[:, cols], preferred_element_type=F32)
        up = jnp.dot(rows[...], up_ref[:, cols], preferred_element_type=F32)
        hidden[:, cols] = (gate / (1.0 + jnp.exp(-gate)) * up).astype(BF16)
        return carry

    lax.fori_loop(0, units // wide, first, 0)

    def second(n, carry):
        cols = pl.ds(pl.multiple_of(n * 512, 512), 512)
        part = jnp.dot(hidden[...], down_ref[:, cols], preferred_element_type=F32).astype(BF16)
        lead = mine_out.shape[:-1]
        mine_out[:, :, :, cols] = part[:half].reshape(*lead, 512)
        peer_out[:, :, :, cols] = part[half:].reshape(*lead, 512)
        return carry

    lax.fori_loop(0, features // 512, second, 0)


def run_expert(mine, peer, gate, up, down):
    features, units = gate.shape
    rows = 2 * mine.size // features
    vmem = pl.BlockSpec(memory_space=pltpu.VMEM)
    return pl.pallas_call(
        expert_kernel,
        in_specs=[vmem] * 5,
        out_shape=[jax.ShapeDtypeStruct(mine.shape, BF16)] * 2,
        scratch_shapes=[pltpu.VMEM((rows, features), BF16), pltpu.VMEM((rows, units), BF16)],
        compiler_params=params(30),
        cost_estimate=pl.CostEstimate(flops=6 * rows * features * units, bytes_accessed=16 << 20, transcendentals=rows * units),
    )(mine, peer, gate, up, down)


def on_device(tokens, expert_ids, route_weights, w_gate, w_up, w_down):
    top = expert_ids.shape[1]
    chips = lax.axis_size("x") * lax.axis_size("y")
    ring = lax.axis_size("z")
    z = lax.axis_index("z").astype(jnp.int32).reshape(1)
    gate, up, down = w_gate[0, 0], w_up[0, 0], w_down[0, 0]

    def along(value, by):
        return lax.ppermute(value, "z", [(i, (i + by) % ring) for i in range(ring)])

    def swap(value):
        return lax.ppermute(value, "core", [(0, 1), (1, 0)])

    def plane(value):
        return lax.all_to_all(value, PLANE, 0, 0, tiled=True)

    own = pl.pallas_call(
        pack_kernel,
        out_shape=jax.ShapeDtypeStruct((tokens.shape[0], tokens.shape[1] + EXTRA), BF16),
    )(tokens, expert_ids, route_weights)
    left1, right1, left2, right2 = along(own, 1), along(own, -1), along(own, 2), along(own, -2)
    left3, right3, opposite = along(left2, 1), along(right2, -1), along(left2, 2)
    near, far = [own, left1, right1, left2, right2], [left3, right3, opposite]

    near_mine = plane(pick(z, near, chips, top))
    far_mine = plane(pick(z, far, chips, top, [near_mine]))
    near_parts = run_expert(near_mine, swap(near_mine), gate, up, down)
    far_parts = run_expert(far_mine, swap(far_mine), gate, up, down)

    far_rows = plane(join(far_parts[0], swap(far_parts[1])))
    far_left, far_right, far_opposite = far_mix(z, far, far_rows, top)
    adds = [along(far_left, -1), along(far_right, 1), along(far_opposite, -2)]
    near_rows = plane(join(near_parts[0], swap(near_parts[1]), [far_left]))
    mix0, mix1, mix2, mix3, mix4 = near_mix(z, near, near_rows, adds, top)
    arrived = [along(mix1, -1), along(mix2, 1), along(mix3, -2), along(mix4, 2)]
    return pl.pallas_call(sum_kernel, out_shape=jax.ShapeDtypeStruct(tokens.shape, BF16))(mix0, *arrived)


def solution(mesh):
    groups, members = mesh.devices.shape
    fine = Mesh(mesh.devices.reshape(groups // 2, 2, 4, members // 4), AXES)
    rows = P(AXES, None)
    weights = P(("y", "core"), ("x", "z"), None, None)
    return jax.shard_map(
        on_device, mesh=fine, in_specs=(rows, rows, rows, weights, weights, weights), out_specs=rows, check_vma=False
    )
```

```python
import functools

import jax
import jax.numpy as jnp
from jax import lax
from jax.experimental import pallas as pl
from jax.experimental.pallas import tpu as pltpu
from jax.sharding import Mesh, PartitionSpec as P

F32, BF16 = jnp.float32, jnp.bfloat16
SLOTS = 2
AXES = ("y", "core", "x", "z")
CHIPS = ("x", "z", "y")
EXTENT = {"y": 4, "x": 4, "z": 8}
WEIGHT = {"y": 32, "x": 8, "z": 1}
CUT = 512
STRIDE = 32
VMEM = pl.BlockSpec(memory_space=pltpu.VMEM)
ANY = pl.BlockSpec(memory_space=pl.ANY)
PICK_MIB = 8
FFN_MIB = 28
LOAD_MIB = 16


def params(mib):
    return pltpu.CompilerParams(vmem_limit_bytes=mib << 20)


def cost(flops, read):
    return pl.CostEstimate(flops=flops, bytes_accessed=read, transcendentals=0)


def expert_at(place):
    expert, inner = 0, 1
    for axis in reversed(CHIPS):
        expert = expert + place // inner % EXTENT[axis] * WEIGHT[axis]
        inner *= EXTENT[axis]
    return expert


def upright(piece):
    size = piece.shape[0]
    same = lax.broadcasted_iota(jnp.int32, (size, size), 0) == lax.broadcasted_iota(jnp.int32, (size, size), 1)
    return lax.dot_general(
        piece.astype(BF16), same.astype(F32).astype(BF16), (((0,), (0,)), ((), ())), preferred_element_type=F32
    )


def slot_parts(ids, lanes):
    tokens, top = ids.shape
    lane = lax.broadcasted_iota(jnp.int32, (tokens, lanes), 1)
    expert = expert_at(lane // SLOTS).astype(F32)
    named = [ids[:, k : k + 1] == expert for k in range(top)]
    hits = functools.reduce(jnp.logical_or, named)
    row = lax.broadcasted_iota(jnp.int32, (tokens, tokens), 0)
    before = lax.broadcasted_iota(jnp.int32, (tokens, tokens), 1) < row
    rank = jnp.dot(before.astype(F32).astype(BF16), hits.astype(F32).astype(BF16), preferred_element_type=F32)
    return named, hits, rank == (lane % SLOTS).astype(F32)


def pick_kernel(ids_ref, tokens_ref, out_ref):
    experts, slots, features = out_ref.shape
    unused, hits, here = slot_parts(upright(ids_ref[...].astype(F32)), experts * slots)
    chosen = (hits & here).astype(F32).astype(BF16)
    for at in range(0, features, CUT):
        cols = slice(at, at + CUT)
        rows = lax.dot_general(chosen, tokens_ref[:, cols], (((0,), (0,)), ((), ())), preferred_element_type=F32)
        out_ref[:, :, cols] = rows.astype(BF16).reshape(experts, slots, CUT)


def table_kernel(ids_ref, weights_ref, unused_ref, out_ref):
    tokens = ids_ref.shape[1]
    named, unused, here = slot_parts(upright(ids_ref[...].astype(F32)), out_ref.shape[1])
    weights = weights_ref[...]
    high = weights.astype(BF16)
    rest = weights - high.astype(F32)
    mid = rest.astype(BF16)
    low = (rest - mid.astype(F32)).astype(BF16)
    out_ref[...] = jnp.zeros_like(out_ref)
    for place, piece in enumerate((high, mid, low)):
        piece = upright(piece.astype(F32))
        value = jnp.zeros(here.shape, F32)
        for k, hit in enumerate(named):
            value = value + jnp.where(hit & here, piece[:, k : k + 1], 0.0)
        out_ref[place * STRIDE : place * STRIDE + tokens] = value.astype(BF16)


def mix_kernel(table_ref, rows_ref, out_ref):
    tokens = out_ref.shape[0]
    experts, slots, features = rows_ref.shape
    tables = [table_ref[place * STRIDE : place * STRIDE + tokens] for place in range(3)]
    for at in range(0, features, CUT):
        rows = rows_ref[:, :, at : at + CUT].reshape(experts * slots, CUT)
        value = sum(jnp.dot(table, rows, preferred_element_type=F32) for table in tables)
        out_ref[:, at : at + CUT] = value.astype(BF16)


def join_kernel(mine_ref, other_ref, unused_ref, out):
    for at in range(0, out.shape[2], CUT):
        parts = [ref[:, :, at : at + CUT].reshape(-1, CUT).astype(F32) for ref in (mine_ref, other_ref)]
        out[:, :, at : at + CUT] = (parts[0] + parts[1]).astype(BF16).reshape(*out.shape[:2], CUT)


def join(mine, other, after):
    return pl.pallas_call(
        join_kernel,
        in_specs=[VMEM] * 2 + [ANY],
        out_shape=jax.ShapeDtypeStruct(mine.shape, BF16),
        compiler_params=params(8),
        cost_estimate=cost(1 << 20, 3 << 20),
    )(mine, other, after)


def expert_kernel(rows_ref, gate, up, down, out_ref, rows, hidden):
    count, features = rows.shape
    units = hidden.shape[1]
    rows[...] = rows_ref[...].reshape(count, features)
    for at in range(0, units, 256):
        cols = slice(at, at + 256)
        gate_act = jnp.dot(rows[...], gate[:, cols], preferred_element_type=F32)
        up_act = jnp.dot(rows[...], up[:, cols], preferred_element_type=F32)
        hidden[:, cols] = (gate_act / (1.0 + jnp.exp(-gate_act)) * up_act).astype(BF16)
    for at in range(0, features, 256):
        cols = slice(at, at + 256)
        part = jnp.dot(hidden[...], down[:, cols], preferred_element_type=F32).astype(BF16)
        out_ref[:, :, cols] = part.reshape(*out_ref.shape[:2], 256)


def load_kernel(*refs):
    count = (len(refs) - 2) // 2
    sources, targets, sems = refs[:count], refs[count + 1 : -1], refs[-1]
    copies = [pltpu.make_async_copy(a, b, sems.at[i]) for i, (a, b) in enumerate(zip(sources, targets))]
    for copy in copies:
        copy.start()
    for copy in copies:
        copy.wait()


def load(values, after):
    return pl.pallas_call(
        load_kernel,
        in_specs=[ANY] * (len(values) + 1),
        out_specs=[VMEM] * len(values),
        out_shape=[jax.ShapeDtypeStruct(v.shape, v.dtype) for v in values],
        scratch_shapes=[pltpu.SemaphoreType.DMA((len(values),))],
        compiler_params=params(LOAD_MIB),
        cost_estimate=cost(0, sum(v.size * 2 for v in values)),
    )(*values, after)


def run_expert(rows, gate, up, down):
    features, units = gate.shape
    count = rows.size // features
    return pl.pallas_call(
        expert_kernel,
        in_specs=[VMEM] * 4,
        out_specs=VMEM,
        out_shape=jax.ShapeDtypeStruct(rows.shape, BF16),
        scratch_shapes=[pltpu.VMEM((count, features), BF16), pltpu.VMEM((count, units), BF16)],
        compiler_params=params(FFN_MIB),
        cost_estimate=pl.CostEstimate(
            flops=6 * count * features * units, bytes_accessed=15 << 20, transcendentals=count * units
        ),
    )(rows, gate, up, down)


def on_device(tokens, expert_ids, route_weights, w_gate, w_up, w_down):
    experts = lax.axis_size("y") * lax.axis_size("x") * lax.axis_size("z")
    ids, weights = expert_ids.T, route_weights.T
    matrices = w_gate[0, 0], w_up[0, 0], w_down[0, 0]

    def swap(value):
        return lax.ppermute(value, "core", [(0, 1), (1, 0)])

    def spread(value):
        return lax.all_to_all(value, CHIPS, 0, 0, tiled=True)

    picked = pl.pallas_call(
        pick_kernel,
        out_shape=jax.ShapeDtypeStruct((experts, SLOTS, tokens.shape[1]), BF16),
        compiler_params=params(PICK_MIB),
        cost_estimate=cost(1 << 28, 4 << 20),
    )(ids, tokens)
    mine = spread(picked)
    peer = swap(mine)
    table = pl.pallas_call(
        table_kernel,
        in_specs=[VMEM] * 2 + [ANY],
        out_shape=jax.ShapeDtypeStruct((3 * STRIDE, experts * SLOTS), BF16),
        compiler_params=params(8),
        cost_estimate=cost(1 << 22, 1 << 18),
    )(ids, weights, mine)
    matrices = matrices[:1] + tuple(load(matrices[1:], mine))
    mine_part = run_expert(mine, *matrices)
    peer_part = run_expert(peer, *matrices)
    returned = spread(join(mine_part, swap(peer_part), table))
    return pl.pallas_call(
        mix_kernel,
        out_shape=jax.ShapeDtypeStruct(tokens.shape, BF16),
        compiler_params=params(8),
        cost_estimate=cost(1 << 29, 4 << 20),
    )(table, returned)


def solution(mesh):
    groups, members = mesh.devices.shape
    fine = Mesh(mesh.devices.reshape(groups // 2, 2, 4, members // 4), AXES)
    rows = P(AXES, None)
    weights = P(("y", "core"), ("x", "z"), None, None)
    return jax.shard_map(
        on_device, mesh=fine, in_specs=(rows, rows, rows, weights, weights, weights), out_specs=rows, check_vma=False
    )
```

```python
import functools

import jax
import jax.numpy as jnp
from jax import lax
from jax.experimental import pallas as pl
from jax.experimental.pallas import tpu as pltpu
from jax.sharding import Mesh, PartitionSpec as P

F32, BF16 = jnp.float32, jnp.bfloat16
SLOTS = 2
AXES = ("y", "core", "x", "z")
BLOCKS = 4
CUT = 512
STRIDE = 32
VMEM = pl.BlockSpec(memory_space=pltpu.VMEM)
SMEM = pl.BlockSpec(memory_space=pltpu.SMEM)
ANY = pl.BlockSpec(memory_space=pl.ANY)
PICK_MIB = 12
FFN_MIB = 28


def params(mib):
    return pltpu.CompilerParams(vmem_limit_bytes=mib << 20)


def cost(flops, read):
    return pl.CostEstimate(flops=flops, bytes_accessed=read, transcendentals=0)


def upright(piece):
    size = piece.shape[0]
    same = lax.broadcasted_iota(jnp.int32, (size, size), 0) == lax.broadcasted_iota(jnp.int32, (size, size), 1)
    return lax.dot_general(
        piece.astype(BF16), same.astype(F32).astype(BF16), (((0,), (0,)), ((), ())), preferred_element_type=F32
    )


def slot_parts(info, planes_ref, lanes, tokens):
    size, top = info.shape[0], info.shape[1] // 2
    lane = lax.broadcasted_iota(jnp.int32, (size, lanes), 1)
    row = lax.broadcasted_iota(jnp.int32, (size, lanes), 0)
    device = lane // (BLOCKS * SLOTS)
    plane = jnp.where(device // 4 % 2 == 0, planes_ref[0], planes_ref[1])
    expert = (device % 4 * 32 + device // 8 * 8 + plane).astype(F32)
    fits = (row // STRIDE == lane // SLOTS % BLOCKS) & (row % STRIDE < tokens)
    named = [(info[:, k : k + 1] == expert) & fits for k in range(top)]
    hits = functools.reduce(jnp.logical_or, named)
    first = lax.broadcasted_iota(jnp.int32, (size, size), 0)
    second = lax.broadcasted_iota(jnp.int32, (size, size), 1)
    before = (first // STRIDE == second // STRIDE) & (second < first)
    rank = jnp.dot(before.astype(F32).astype(BF16), hits.astype(F32).astype(BF16), preferred_element_type=F32)
    return named, hits, rank == (lane % SLOTS).astype(F32)


def gather_info(infos, scratch):
    scratch[...] = jnp.zeros_like(scratch)
    for b, ref in enumerate(infos):
        value = ref[...]
        high = value.astype(BF16)
        rest = value - high.astype(F32)
        mid = rest.astype(BF16)
        low = (rest - mid.astype(F32)).astype(BF16)
        for place, piece in enumerate((high, mid, low)):
            scratch[place, b * STRIDE : b * STRIDE + value.shape[1]] = upright(piece)


def pick_kernel(planes_ref, *refs):
    infos, blocks, (out_ref, info, table) = refs[:BLOCKS], refs[BLOCKS : 2 * BLOCKS], refs[2 * BLOCKS :]
    tokens = blocks[0].shape[0]
    devices, each, features = out_ref.shape
    table[...] = jnp.zeros_like(table)
    for b, block in enumerate(blocks):
        table[b * STRIDE : b * STRIDE + tokens] = block[...]
    gather_info(infos, info)
    unused, hits, here = slot_parts(info[0], planes_ref, devices * each, tokens)
    chosen = (hits & here).astype(F32).astype(BF16)
    for at in range(0, features, CUT):
        cols = slice(at, at + CUT)
        rows = lax.dot_general(chosen, table[:, cols], (((0,), (0,)), ((), ())), preferred_element_type=F32)
        out_ref[:, :, cols] = rows.astype(BF16).reshape(devices, each, CUT)


def pick(planes, infos, blocks, devices):
    tokens, features = blocks[0].shape
    return pl.pallas_call(
        pick_kernel,
        in_specs=[SMEM] + [VMEM] * (2 * BLOCKS),
        out_shape=jax.ShapeDtypeStruct((devices, BLOCKS * SLOTS, features), BF16),
        scratch_shapes=[
            pltpu.VMEM((3, BLOCKS * STRIDE, infos[0].shape[0]), F32),
            pltpu.VMEM((BLOCKS * STRIDE, features), BF16),
        ],
        compiler_params=params(PICK_MIB),
        cost_estimate=cost(1 << 35, 4 << 20),
    )(planes, *infos, *blocks)


def table_kernel(planes_ref, *refs):
    infos, (out_ref, info) = refs[:BLOCKS], refs[BLOCKS + 1 :]
    gather_info(infos, info)
    named, unused, here = slot_parts(info[0], planes_ref, out_ref.shape[2], infos[0].shape[1])
    top = len(named)
    for place in range(3):
        value = jnp.zeros(here.shape, F32)
        for k, hit in enumerate(named):
            value = value + jnp.where(hit & here, info[place, :, top + k : top + k + 1], 0.0)
        out_ref[place] = value.astype(BF16)


def make_table(planes, infos, devices, after):
    return pl.pallas_call(
        table_kernel,
        in_specs=[SMEM] + [VMEM] * BLOCKS + [ANY],
        out_shape=jax.ShapeDtypeStruct((3, BLOCKS * STRIDE, devices * BLOCKS * SLOTS), BF16),
        scratch_shapes=[pltpu.VMEM((3, BLOCKS * STRIDE, infos[0].shape[0]), F32)],
        compiler_params=params(8),
        cost_estimate=cost(1 << 22, 1 << 18),
    )(planes, *infos, after)


def mix_kernel(table_ref, rows_ref, *outs):
    tokens = outs[0].shape[0]
    devices, each, features = rows_ref.shape
    for at in range(0, features, CUT):
        cols = slice(at, at + CUT)
        rows = rows_ref[:, :, cols].reshape(devices * each, CUT)
        total = sum(jnp.dot(table_ref[place], rows, preferred_element_type=F32) for place in range(3))
        for b, out in enumerate(outs):
            out[:, cols] = total[b * STRIDE : b * STRIDE + tokens].astype(out.dtype)


def sum_kernel(own, *refs):
    total = own[...]
    for ref in refs[:-1]:
        total = total + ref[...].astype(F32)
    refs[-1][...] = total.astype(BF16)


def join_kernel(mine_ref, other_ref, unused_ref, out):
    for at in range(0, out.shape[2], CUT):
        parts = [ref[:, :, at : at + CUT].reshape(-1, CUT).astype(F32) for ref in (mine_ref, other_ref)]
        out[:, :, at : at + CUT] = (parts[0] + parts[1]).astype(BF16).reshape(*out.shape[:2], CUT)


def join(mine, other, after):
    return pl.pallas_call(
        join_kernel,
        in_specs=[VMEM] * 2 + [ANY],
        out_shape=jax.ShapeDtypeStruct(mine.shape, BF16),
        compiler_params=params(8),
        cost_estimate=cost(1 << 20, 3 << 20),
    )(mine, other, after)


def expert_kernel(rows_ref, gate, up, down, out_ref, rows, hidden):
    count, features = rows.shape
    units = hidden.shape[1]
    rows[...] = rows_ref[...].reshape(count, features)
    for at in range(0, units, 256):
        cols = slice(at, at + 256)
        gate_act = jnp.dot(rows[...], gate[:, cols], preferred_element_type=F32)
        up_act = jnp.dot(rows[...], up[:, cols], preferred_element_type=F32)
        hidden[:, cols] = (gate_act / (1.0 + jnp.exp(-gate_act)) * up_act).astype(BF16)
    for at in range(0, features, 256):
        cols = slice(at, at + 256)
        part = jnp.dot(hidden[...], down[:, cols], preferred_element_type=F32).astype(BF16)
        out_ref[:, :, cols] = part.reshape(*out_ref.shape[:2], 256)


def run_expert(rows, gate, up, down):
    features, units = gate.shape
    count = rows.size // features
    return pl.pallas_call(
        expert_kernel,
        in_specs=[VMEM] * 4,
        out_specs=VMEM,
        out_shape=jax.ShapeDtypeStruct(rows.shape, BF16),
        scratch_shapes=[pltpu.VMEM((count, features), BF16), pltpu.VMEM((count, units), BF16)],
        compiler_params=params(FFN_MIB),
        cost_estimate=pl.CostEstimate(
            flops=6 * count * features * units, bytes_accessed=15 << 20, transcendentals=count * units
        ),
    )(rows, gate, up, down)


def on_device(tokens, expert_ids, route_weights, w_gate, w_up, w_down):
    ring, depth, width = lax.axis_size("z"), lax.axis_size("x"), lax.axis_size("y")
    matrices = w_gate[0, 0], w_up[0, 0], w_down[0, 0]
    core, z = lax.axis_index("core"), lax.axis_index("z")
    pair = (z - core + ring) % ring // 2
    planes = jnp.stack([(2 * pair + member + core) % ring for member in range(2)]).astype(jnp.int32)

    def route(by, back):
        pairs = []
        for c in range(2):
            for s in range(ring):
                t = s + by if (s + by) % 2 == 0 else s - by
                pairs.append((c * ring + (s + c) % ring, c * ring + (t + c) % ring))
        return [(b, a) for a, b in pairs] if back else pairs

    def send(value, by, back=False):
        return lax.ppermute(value, ("core", "z"), route(by, back))

    groups = [
        [
            ((y * 2 + c) * depth + x) * ring + (2 * p + member + c) % ring
            for x in range(depth)
            for member in range(2)
            for y in range(width)
        ]
        for c in range(2)
        for p in range(ring // 2)
    ]

    def spread(value):
        return lax.all_to_all(value, AXES, 0, 0, axis_index_groups=groups, tiled=True)

    def swap(value):
        return lax.ppermute(value, "core", [(0, 1), (1, 0)])

    info = jnp.concatenate([expert_ids.T.astype(F32), route_weights.T], axis=0)
    blocks, infos = [tokens], [info]
    blocks += [send(tokens, by) for by in range(1, BLOCKS)]
    infos += [send(info, by) for by in range(1, BLOCKS)]
    devices = 2 * depth * width
    mine = spread(pick(planes, infos, blocks, devices))
    peer = swap(mine)
    table = make_table(planes, infos, devices, mine)
    mine_part = run_expert(mine, *matrices)
    peer_part = run_expert(peer, *matrices)
    returned = spread(join(mine_part, swap(peer_part), table))
    shape = tokens.shape
    own, *others = pl.pallas_call(
        mix_kernel,
        out_shape=[jax.ShapeDtypeStruct(shape, F32)] + [jax.ShapeDtypeStruct(shape, BF16)] * (BLOCKS - 1),
        compiler_params=params(8),
        cost_estimate=cost(1 << 29, 4 << 20),
    )(table, returned)
    arrived = [send(value, by, True) for by, value in enumerate(others, 1)]
    return pl.pallas_call(
        sum_kernel, out_shape=jax.ShapeDtypeStruct(shape, BF16), compiler_params=params(8)
    )(own, *arrived)


def solution(mesh):
    groups, members = mesh.devices.shape
    fine = Mesh(mesh.devices.reshape(groups // 2, 2, 4, members // 4), AXES)
    rows = P(AXES, None)
    weights = P(("y", "core"), ("x", "z"), None, None)
    return jax.shard_map(
        on_device, mesh=fine, in_specs=(rows, rows, rows, weights, weights, weights), out_specs=rows, check_vma=False
    )
```

```python
import functools

import jax
import jax.numpy as jnp
from jax import lax
from jax.experimental import pallas as pl
from jax.experimental.pallas import tpu as pltpu
from jax.sharding import Mesh, PartitionSpec as P

F32, BF16 = jnp.float32, jnp.bfloat16
SLOTS = 2
AXES = ("y", "core", "x", "z")
BLOCKS = 4
CUT = 512
STRIDE = 32
VMEM = pl.BlockSpec(memory_space=pltpu.VMEM)
SMEM = pl.BlockSpec(memory_space=pltpu.SMEM)
ANY = pl.BlockSpec(memory_space=pl.ANY)
PICK_MIB = 12
PREPARE_MIB = 8
FFN_MIB = 28


def params(mib):
    return pltpu.CompilerParams(vmem_limit_bytes=mib << 20)


def cost(flops, read):
    return pl.CostEstimate(flops=flops, bytes_accessed=read, transcendentals=0)


def upright(piece):
    size = piece.shape[0]
    same = lax.broadcasted_iota(jnp.int32, (size, size), 0) == lax.broadcasted_iota(jnp.int32, (size, size), 1)
    return lax.dot_general(
        piece.astype(BF16), same.astype(F32).astype(BF16), (((0,), (0,)), ((), ())), preferred_element_type=F32
    )


def slot_parts(info, planes_ref, lanes, tokens):
    size, top = info.shape[0], info.shape[1] // 2
    lane = lax.broadcasted_iota(jnp.int32, (size, lanes), 1)
    row = lax.broadcasted_iota(jnp.int32, (size, lanes), 0)
    device = lane // (BLOCKS * SLOTS)
    plane = jnp.where(device // 1 % 2 == 0, planes_ref[0], planes_ref[1])
    expert = (device // 2 % 4 * 32 + device // 8 % 4 * 8 + plane).astype(F32)
    fits = (row // STRIDE == lane // SLOTS % BLOCKS) & (row % STRIDE < tokens)
    named = [(info[:, k : k + 1] == expert) & fits for k in range(top)]
    hits = functools.reduce(jnp.logical_or, named)
    first = lax.broadcasted_iota(jnp.int32, (size, size), 0)
    second = lax.broadcasted_iota(jnp.int32, (size, size), 1)
    before = (first // STRIDE == second // STRIDE) & (second < first)
    rank = jnp.dot(before.astype(F32).astype(BF16), hits.astype(F32).astype(BF16), preferred_element_type=F32)
    return named, hits, rank == (lane % SLOTS).astype(F32)


def gather_info(infos, scratch, terms):
    scratch[...] = jnp.zeros_like(scratch)
    for b, ref in enumerate(infos):
        value = ref[...]
        high = value.astype(BF16)
        rest = value - high.astype(F32)
        mid = rest.astype(BF16)
        low = (rest - mid.astype(F32)).astype(BF16)
        for place, piece in enumerate((high, mid, low)[:terms]):
            scratch[place, b * STRIDE : b * STRIDE + value.shape[1]] = upright(piece)


def prepare_kernel(ids_ref, weights_ref, tokens_ref, info_ref, own_ref):
    top = ids_ref.shape[0]
    info_ref[:top] = ids_ref[...].astype(F32)
    info_ref[top:] = weights_ref[...]
    own_ref[...] = tokens_ref[...]


def prepare(ids, weights, tokens):
    return pl.pallas_call(
        prepare_kernel,
        out_shape=[
            jax.ShapeDtypeStruct((2 * ids.shape[0], ids.shape[1]), F32),
            jax.ShapeDtypeStruct(tokens.shape, BF16),
        ],
        compiler_params=params(PREPARE_MIB),
        cost_estimate=cost(0, 1 << 18),
    )(ids, weights, tokens)


def choose_kernel(planes_ref, *refs):
    infos, (chosen_ref, info) = refs[:BLOCKS], refs[BLOCKS:]
    gather_info(infos, info, 1)
    unused, hits, here = slot_parts(info[0], planes_ref, chosen_ref.shape[1], infos[0].shape[1])
    chosen_ref[...] = (hits & here).astype(F32).astype(BF16)


def table_kernel(planes_ref, *refs):
    infos, (table_ref, info) = refs[:BLOCKS], refs[BLOCKS + 1 :]
    gather_info(infos, info, 3)
    named, unused, here = slot_parts(info[0], planes_ref, table_ref.shape[2], infos[0].shape[1])
    top = len(named)
    for place in range(3):
        value = jnp.zeros(here.shape, F32)
        for k, hit in enumerate(named):
            value = value + jnp.where(hit & here, info[place, :, top + k : top + k + 1], 0.0)
        table_ref[place] = value.astype(BF16)


def from_info(kernel, terms, lead, planes, infos, devices, after=()):
    return pl.pallas_call(
        kernel,
        in_specs=[SMEM] + [VMEM] * BLOCKS + [ANY] * len(after),
        out_shape=jax.ShapeDtypeStruct((*lead, BLOCKS * STRIDE, devices * BLOCKS * SLOTS), BF16),
        scratch_shapes=[pltpu.VMEM((terms, BLOCKS * STRIDE, infos[0].shape[0]), F32)],
        compiler_params=params(8),
        cost_estimate=cost(1 << 22, 1 << 18),
    )(planes, *infos, *after)


def pick_kernel(chosen_ref, *refs):
    blocks, (out_ref, table) = refs[:BLOCKS], refs[BLOCKS:]
    tokens = blocks[0].shape[0]
    devices, each, features = out_ref.shape
    table[...] = jnp.zeros_like(table)
    for b, block in enumerate(blocks):
        table[b * STRIDE : b * STRIDE + tokens] = block[...]
    for at in range(0, features, CUT):
        cols = slice(at, at + CUT)
        rows = lax.dot_general(
            chosen_ref[...], table[:, cols], (((0,), (0,)), ((), ())), preferred_element_type=F32
        )
        out_ref[:, :, cols] = rows.astype(BF16).reshape(devices, each, CUT)


def pick(chosen, blocks, devices):
    features = blocks[0].shape[1]
    return pl.pallas_call(
        pick_kernel,
        out_shape=jax.ShapeDtypeStruct((devices, BLOCKS * SLOTS, features), BF16),
        scratch_shapes=[pltpu.VMEM((BLOCKS * STRIDE, features), BF16)],
        compiler_params=params(PICK_MIB),
        cost_estimate=cost(1 << 35, 4 << 20),
    )(chosen, *blocks)


def mix_kernel(table_ref, rows_ref, *outs):
    tokens = outs[0].shape[0]
    devices, each, features = rows_ref.shape
    for at in range(0, features, CUT):
        cols = slice(at, at + CUT)
        rows = rows_ref[:, :, cols].reshape(devices * each, CUT)
        total = sum(jnp.dot(table_ref[place], rows, preferred_element_type=F32) for place in range(3))
        for b, out in enumerate(outs):
            out[:, cols] = total[b * STRIDE : b * STRIDE + tokens].astype(out.dtype)


def sum_kernel(own, *refs):
    total = own[...]
    for ref in refs[:-1]:
        total = total + ref[...].astype(F32)
    refs[-1][...] = total.astype(BF16)


def join_kernel(mine_ref, other_ref, out):
    for at in range(0, out.shape[2], CUT):
        parts = [ref[:, :, at : at + CUT].reshape(-1, CUT).astype(F32) for ref in (mine_ref, other_ref)]
        out[:, :, at : at + CUT] = (parts[0] + parts[1]).astype(BF16).reshape(*out.shape[:2], CUT)


def join(mine, other):
    return pl.pallas_call(
        join_kernel,
        out_shape=jax.ShapeDtypeStruct(mine.shape, BF16),
        compiler_params=params(8),
        cost_estimate=cost(1 << 20, 3 << 20),
    )(mine, other)


def expert_kernel(rows_ref, gate, up, down, *refs):
    out_ref, rows, hidden = refs[-3:]
    count, features = rows.shape
    units = hidden.shape[1]
    rows[...] = rows_ref[...].reshape(count, features)
    for at in range(0, units, 256):
        cols = slice(at, at + 256)
        gate_act = jnp.dot(rows[...], gate[:, cols], preferred_element_type=F32)
        up_act = jnp.dot(rows[...], up[:, cols], preferred_element_type=F32)
        hidden[:, cols] = (gate_act / (1.0 + jnp.exp(-gate_act)) * up_act).astype(BF16)
    for at in range(0, features, 256):
        cols = slice(at, at + 256)
        part = jnp.dot(hidden[...], down[:, cols], preferred_element_type=F32).astype(BF16)
        out_ref[:, :, cols] = part.reshape(*out_ref.shape[:2], 256)


def run_expert(rows, gate, up, down, after=()):
    features, units = gate.shape
    count = rows.size // features
    return pl.pallas_call(
        expert_kernel,
        in_specs=[VMEM] * 4 + [ANY] * len(after),
        out_specs=VMEM,
        out_shape=jax.ShapeDtypeStruct(rows.shape, BF16),
        scratch_shapes=[pltpu.VMEM((count, features), BF16), pltpu.VMEM((count, units), BF16)],
        compiler_params=params(FFN_MIB),
        cost_estimate=pl.CostEstimate(
            flops=6 * count * features * units, bytes_accessed=15 << 20, transcendentals=count * units
        ),
    )(rows, gate, up, down, *after)


def on_device(tokens, expert_ids, route_weights, w_gate, w_up, w_down):
    ring, depth, width = lax.axis_size("z"), lax.axis_size("x"), lax.axis_size("y")
    matrices = w_gate[0, 0], w_up[0, 0], w_down[0, 0]
    core, z = lax.axis_index("core"), lax.axis_index("z")
    pair = (z - core + ring) % ring // 2
    planes = jnp.stack([(2 * pair + member + core) % ring for member in range(2)]).astype(jnp.int32)

    def route(by, back):
        pairs = []
        for c in range(2):
            for s in range(ring):
                t = s + by if (s + by) % 2 == 0 else s - by
                pairs.append((c * ring + (s + c) % ring, c * ring + (t + c) % ring))
        return [(b, a) for a, b in pairs] if back else pairs

    def send(value, by, back=False):
        return lax.ppermute(value, ("core", "z"), route(by, back))

    groups = [
        [
            ((y * 2 + c) * depth + x) * ring + (2 * p + member + c) % ring
            for x in range(depth)
            for y in range(width)
            for member in range(2)
        ]
        for c in range(2)
        for p in range(ring // 2)
    ]

    def spread(value):
        return lax.all_to_all(value, AXES, 0, 0, axis_index_groups=groups, tiled=True)

    def swap(value):
        return lax.ppermute(value, "core", [(0, 1), (1, 0)])

    info, own = prepare(expert_ids.T, route_weights.T, tokens)
    blocks, infos = [tokens], [info]
    blocks += [send(tokens, by) for by in range(1, BLOCKS)]
    infos += [send(info, by) for by in range(1, BLOCKS)]
    devices = 2 * depth * width
    chosen = from_info(choose_kernel, 1, (), planes, infos, devices)
    mine = spread(pick(chosen, [own] + blocks[1:], devices))
    peer = swap(mine)
    table = from_info(table_kernel, 3, (3,), planes, infos, devices, [mine])
    mine_part = run_expert(mine, *matrices)
    peer_part = run_expert(peer, *matrices, [table])
    returned = spread(join(mine_part, swap(peer_part)))
    shape = tokens.shape
    own, *others = pl.pallas_call(
        mix_kernel,
        out_shape=[jax.ShapeDtypeStruct(shape, F32)] + [jax.ShapeDtypeStruct(shape, BF16)] * (BLOCKS - 1),
        compiler_params=params(8),
        cost_estimate=cost(1 << 29, 4 << 20),
    )(table, returned)
    arrived = [send(value, by, True) for by, value in enumerate(others, 1)]
    return pl.pallas_call(
        sum_kernel, out_shape=jax.ShapeDtypeStruct(shape, BF16), compiler_params=params(8)
    )(own, *arrived)


def solution(mesh):
    groups, members = mesh.devices.shape
    fine = Mesh(mesh.devices.reshape(groups // 2, 2, 4, members // 4), AXES)
    rows = P(AXES, None)
    weights = P(("y", "core"), ("x", "z"), None, None)
    return jax.shard_map(
        on_device, mesh=fine, in_specs=(rows, rows, rows, weights, weights, weights), out_specs=rows, check_vma=False
    )
```

```python
import functools

import jax
import jax.numpy as jnp
from jax import lax
from jax.experimental import pallas as pl
from jax.experimental.pallas import tpu as pltpu
from jax.sharding import Mesh, PartitionSpec as P

F32, BF16 = jnp.float32, jnp.bfloat16
SLOTS = 2
AXES = ("y", "core", "x", "z")
BLOCKS = 4
INFOS = 3
CUT = 512
STRIDE = 32
VMEM = pl.BlockSpec(memory_space=pltpu.VMEM)
SMEM = pl.BlockSpec(memory_space=pltpu.SMEM)
ANY = pl.BlockSpec(memory_space=pl.ANY)
PICK_MIB = 12
PREPARE_MIB = 8
FFN_MIB = 28


def params(mib):
    return pltpu.CompilerParams(vmem_limit_bytes=mib << 20)


def cost(flops, read):
    return pl.CostEstimate(flops=flops, bytes_accessed=read, transcendentals=0)


def upright(piece):
    size = piece.shape[0]
    same = lax.broadcasted_iota(jnp.int32, (size, size), 0) == lax.broadcasted_iota(jnp.int32, (size, size), 1)
    return lax.dot_general(
        piece.astype(BF16), same.astype(F32).astype(BF16), (((0,), (0,)), ((), ())), preferred_element_type=F32
    )


def slot_parts(info, planes_ref, lanes, tokens):
    size, top = info.shape[0], info.shape[1] // 2
    lane = lax.broadcasted_iota(jnp.int32, (size, lanes), 1)
    row = lax.broadcasted_iota(jnp.int32, (size, lanes), 0)
    device = lane // (BLOCKS * SLOTS)
    plane = jnp.where(device // 1 % 2 == 0, planes_ref[0], planes_ref[1])
    expert = (device // 2 % 4 * 32 + device // 8 % 4 * 8 + plane).astype(F32)
    fits = (row // STRIDE == lane // SLOTS % BLOCKS) & (row % STRIDE < tokens)
    named = [(info[:, k : k + 1] == expert) & fits for k in range(top)]
    hits = functools.reduce(jnp.logical_or, named)
    first = lax.broadcasted_iota(jnp.int32, (size, size), 0)
    second = lax.broadcasted_iota(jnp.int32, (size, size), 1)
    before = (first // STRIDE == second // STRIDE) & (second < first)
    rank = jnp.dot(before.astype(F32).astype(BF16), hits.astype(F32).astype(BF16), preferred_element_type=F32)
    return named, hits, rank == (lane % SLOTS).astype(F32)


def gather_info(infos, scratch, terms):
    scratch[...] = jnp.zeros_like(scratch)
    size = infos[0].shape[0]
    for b, value in enumerate((infos[0][...], infos[1][...], infos[2][:size], infos[2][size:])):
        high = value.astype(BF16)
        rest = value - high.astype(F32)
        mid = rest.astype(BF16)
        low = (rest - mid.astype(F32)).astype(BF16)
        for place, piece in enumerate((high, mid, low)[:terms]):
            scratch[place, b * STRIDE : b * STRIDE + value.shape[1]] = upright(piece)


def prepare_kernel(ids_ref, weights_ref, tokens_ref, info_ref, own_ref):
    top = ids_ref.shape[0]
    info_ref[:top] = ids_ref[...].astype(F32)
    info_ref[top:] = weights_ref[...]
    own_ref[...] = tokens_ref[...]


def prepare(ids, weights, tokens):
    return pl.pallas_call(
        prepare_kernel,
        out_shape=[
            jax.ShapeDtypeStruct((2 * ids.shape[0], ids.shape[1]), F32),
            jax.ShapeDtypeStruct(tokens.shape, BF16),
        ],
        compiler_params=params(PREPARE_MIB),
        cost_estimate=cost(0, 1 << 18),
    )(ids, weights, tokens)


def choose_kernel(planes_ref, *refs):
    infos, (chosen_ref, info) = refs[:INFOS], refs[INFOS:]
    gather_info(infos, info, 1)
    unused, hits, here = slot_parts(info[0], planes_ref, chosen_ref.shape[1], infos[0].shape[1])
    chosen_ref[...] = (hits & here).astype(F32).astype(BF16)


def table_kernel(planes_ref, *refs):
    infos, (table_ref, info) = refs[:INFOS], refs[INFOS + 1 :]
    gather_info(infos, info, 3)
    named, unused, here = slot_parts(info[0], planes_ref, table_ref.shape[2], infos[0].shape[1])
    top = len(named)
    for place in range(3):
        value = jnp.zeros(here.shape, F32)
        for k, hit in enumerate(named):
            value = value + jnp.where(hit & here, info[place, :, top + k : top + k + 1], 0.0)
        table_ref[place] = value.astype(BF16)


def from_info(kernel, terms, lead, planes, infos, devices, after=()):
    return pl.pallas_call(
        kernel,
        in_specs=[SMEM] + [VMEM] * INFOS + [ANY] * len(after),
        out_shape=jax.ShapeDtypeStruct((*lead, BLOCKS * STRIDE, devices * BLOCKS * SLOTS), BF16),
        scratch_shapes=[pltpu.VMEM((terms, BLOCKS * STRIDE, infos[0].shape[0]), F32)],
        compiler_params=params(8),
        cost_estimate=cost(1 << 22, 1 << 18),
    )(planes, *infos, *after)


def pick_kernel(chosen_ref, *refs):
    blocks, (out_ref, table) = refs[:BLOCKS], refs[BLOCKS:]
    tokens = blocks[0].shape[0]
    devices, each, features = out_ref.shape
    table[...] = jnp.zeros_like(table)
    for b, block in enumerate(blocks):
        table[b * STRIDE : b * STRIDE + tokens] = block[...]
    for at in range(0, features, CUT):
        cols = slice(at, at + CUT)
        rows = lax.dot_general(
            chosen_ref[...], table[:, cols], (((0,), (0,)), ((), ())), preferred_element_type=F32
        )
        out_ref[:, :, cols] = rows.astype(BF16).reshape(devices, each, CUT)


def pick(chosen, blocks, devices):
    features = blocks[0].shape[1]
    return pl.pallas_call(
        pick_kernel,
        out_shape=jax.ShapeDtypeStruct((devices, BLOCKS * SLOTS, features), BF16),
        scratch_shapes=[pltpu.VMEM((BLOCKS * STRIDE, features), BF16)],
        compiler_params=params(PICK_MIB),
        cost_estimate=cost(1 << 35, 4 << 20),
    )(chosen, *blocks)


def mix_kernel(table_ref, rows_ref, *outs):
    tokens = outs[0].shape[0]
    devices, each, features = rows_ref.shape
    for at in range(0, features, CUT):
        cols = slice(at, at + CUT)
        rows = rows_ref[:, :, cols].reshape(devices * each, CUT)
        total = sum(jnp.dot(table_ref[place], rows, preferred_element_type=F32) for place in range(3))
        for b, out in enumerate(outs):
            out[:, cols] = total[b * STRIDE : b * STRIDE + tokens].astype(out.dtype)


def sum_kernel(own, *refs):
    total = own[...]
    for ref in refs[:-1]:
        total = total + ref[...].astype(F32)
    refs[-1][...] = total.astype(BF16)


def join_kernel(mine_ref, other_ref, out):
    for at in range(0, out.shape[2], CUT):
        parts = [ref[:, :, at : at + CUT].reshape(-1, CUT).astype(F32) for ref in (mine_ref, other_ref)]
        out[:, :, at : at + CUT] = (parts[0] + parts[1]).astype(BF16).reshape(*out.shape[:2], CUT)


def join(mine, other):
    return pl.pallas_call(
        join_kernel,
        out_shape=jax.ShapeDtypeStruct(mine.shape, BF16),
        compiler_params=params(8),
        cost_estimate=cost(1 << 20, 3 << 20),
    )(mine, other)


def expert_kernel(rows_ref, gate, up, down, *refs):
    out_ref, rows, hidden = refs[-3:]
    count, features = rows.shape
    units = hidden.shape[1]
    rows[...] = rows_ref[...].reshape(count, features)
    for at in range(0, units, 256):
        cols = slice(at, at + 256)
        gate_act = jnp.dot(rows[...], gate[:, cols], preferred_element_type=F32)
        up_act = jnp.dot(rows[...], up[:, cols], preferred_element_type=F32)
        hidden[:, cols] = (gate_act / (1.0 + jnp.exp(-gate_act)) * up_act).astype(BF16)
    for at in range(0, features, 256):
        cols = slice(at, at + 256)
        part = jnp.dot(hidden[...], down[:, cols], preferred_element_type=F32).astype(BF16)
        out_ref[:, :, cols] = part.reshape(*out_ref.shape[:2], 256)


def run_expert(rows, gate, up, down, after=()):
    features, units = gate.shape
    count = rows.size // features
    return pl.pallas_call(
        expert_kernel,
        in_specs=[VMEM] * 4 + [ANY] * len(after),
        out_specs=VMEM,
        out_shape=jax.ShapeDtypeStruct(rows.shape, BF16),
        scratch_shapes=[pltpu.VMEM((count, features), BF16), pltpu.VMEM((count, units), BF16)],
        compiler_params=params(FFN_MIB),
        cost_estimate=pl.CostEstimate(
            flops=6 * count * features * units, bytes_accessed=15 << 20, transcendentals=count * units
        ),
    )(rows, gate, up, down, *after)


def on_device(tokens, expert_ids, route_weights, w_gate, w_up, w_down):
    ring, depth, width = lax.axis_size("z"), lax.axis_size("x"), lax.axis_size("y")
    matrices = w_gate[0, 0], w_up[0, 0], w_down[0, 0]
    core, z = lax.axis_index("core"), lax.axis_index("z")
    pair = (z - core + ring) % ring // 2
    planes = jnp.stack([(2 * pair + member + core) % ring for member in range(2)]).astype(jnp.int32)

    def route(by, back):
        pairs = []
        for c in range(2):
            for s in range(ring):
                t = s + by if (s + by) % 2 == 0 else s - by
                pairs.append((c * ring + (s + c) % ring, c * ring + (t + c) % ring))
        return [(b, a) for a, b in pairs] if back else pairs

    def send(value, by, back=False):
        return lax.ppermute(value, ("core", "z"), route(by, back))

    groups = [
        [
            ((y * 2 + c) * depth + x) * ring + (2 * p + member + c) % ring
            for x in range(depth)
            for y in range(width)
            for member in range(2)
        ]
        for c in range(2)
        for p in range(ring // 2)
    ]

    def spread(value):
        return lax.all_to_all(value, AXES, 0, 0, axis_index_groups=groups, tiled=True)

    def swap(value):
        return lax.ppermute(value, "core", [(0, 1), (1, 0)])

    info, own = prepare(expert_ids.T, route_weights.T, tokens)
    blocks, infos = [tokens], [info]
    blocks += [send(tokens, 1), send(tokens, 2)]
    blocks += [send(blocks[1], 2)]
    infos += [send(info, 1)]
    infos += [send(jnp.concatenate(infos, axis=0), 2)]
    devices = 2 * depth * width
    chosen = from_info(choose_kernel, 1, (), planes, infos, devices)
    mine = spread(pick(chosen, [own] + blocks[1:], devices))
    peer = swap(mine)
    table = from_info(table_kernel, 3, (3,), planes, infos, devices, [mine])
    mine_part = run_expert(mine, *matrices)
    peer_part = run_expert(peer, *matrices, [table])
    returned = spread(join(mine_part, swap(peer_part)))
    shape = tokens.shape
    own, next1, next2, next3 = pl.pallas_call(
        mix_kernel,
        out_shape=[jax.ShapeDtypeStruct(shape, t) for t in (F32, F32, BF16, BF16)],
        compiler_params=params(8),
        cost_estimate=cost(1 << 29, 4 << 20),
    )(table, returned)

    def add(*parts):
        return pl.pallas_call(
            sum_kernel, out_shape=jax.ShapeDtypeStruct(shape, BF16), compiler_params=params(8)
        )(*parts)

    next2, next3 = send(next2, 2, True), send(next3, 2, True)
    return add(own, next2, send(add(next1, next3), 1, True))


def solution(mesh):
    groups, members = mesh.devices.shape
    fine = Mesh(mesh.devices.reshape(groups // 2, 2, 4, members // 4), AXES)
    rows = P(AXES, None)
    weights = P(("y", "core"), ("x", "z"), None, None)
    return jax.shard_map(
        on_device, mesh=fine, in_specs=(rows, rows, rows, weights, weights, weights), out_specs=rows, check_vma=False
    )
```

```python
import functools

import jax
import jax.numpy as jnp
from jax import lax
from jax.experimental import pallas as pl
from jax.experimental.pallas import tpu as pltpu
from jax.sharding import Mesh, PartitionSpec as P

F32, BF16 = jnp.float32, jnp.bfloat16
SLOTS = 2
AXES = ("y", "core", "x", "z")
BLOCKS = 4
INFOS = 3
CUT = 512
STRIDE = 32
VMEM = pl.BlockSpec(memory_space=pltpu.VMEM)
SMEM = pl.BlockSpec(memory_space=pltpu.SMEM)
ANY = pl.BlockSpec(memory_space=pl.ANY)
PICK_MIB = 12
PREPARE_MIB = 8
FFN_MIB = 28


def params(mib):
    return pltpu.CompilerParams(vmem_limit_bytes=mib << 20)


def cost(flops, read):
    return pl.CostEstimate(flops=flops, bytes_accessed=read, transcendentals=0)


def upright(piece):
    size = piece.shape[0]
    same = lax.broadcasted_iota(jnp.int32, (size, size), 0) == lax.broadcasted_iota(jnp.int32, (size, size), 1)
    return lax.dot_general(
        piece.astype(BF16), same.astype(F32).astype(BF16), (((0,), (0,)), ((), ())), preferred_element_type=F32
    )


def slot_parts(info, planes_ref, lanes, tokens):
    size, top = info.shape[0], info.shape[1] // 2
    lane = lax.broadcasted_iota(jnp.int32, (size, lanes), 1)
    row = lax.broadcasted_iota(jnp.int32, (size, lanes), 0)
    device = lane // (BLOCKS * SLOTS)
    plane = jnp.where(device // 1 % 2 == 0, planes_ref[0], planes_ref[1])
    expert = (device // 2 % 4 * 32 + device // 8 % 4 * 8 + plane).astype(F32)
    fits = (row // STRIDE == lane // SLOTS % BLOCKS) & (row % STRIDE < tokens)
    named = [(info[:, k : k + 1] == expert) & fits for k in range(top)]
    hits = functools.reduce(jnp.logical_or, named)
    first = lax.broadcasted_iota(jnp.int32, (size, size), 0)
    second = lax.broadcasted_iota(jnp.int32, (size, size), 1)
    before = (first // STRIDE == second // STRIDE) & (second < first)
    rank = jnp.dot(before.astype(F32).astype(BF16), hits.astype(F32).astype(BF16), preferred_element_type=F32)
    return named, hits, rank == (lane % SLOTS).astype(F32)


def gather_info(infos, scratch, terms):
    scratch[...] = jnp.zeros_like(scratch)
    size = infos[0].shape[0]
    for b, value in enumerate((infos[0][...], infos[1][...], infos[2][:size], infos[2][size:])):
        high = value.astype(BF16)
        rest = value - high.astype(F32)
        mid = rest.astype(BF16)
        low = (rest - mid.astype(F32)).astype(BF16)
        for place, piece in enumerate((high, mid, low)[:terms]):
            scratch[place, b * STRIDE : b * STRIDE + value.shape[1]] = upright(piece)


def prepare_kernel(ids_ref, weights_ref, info_ref):
    top = ids_ref.shape[0]
    info_ref[:top] = ids_ref[...].astype(F32)
    info_ref[top:] = weights_ref[...]


def prepare(ids, weights):
    return pl.pallas_call(
        prepare_kernel,
        out_shape=jax.ShapeDtypeStruct((2 * ids.shape[0], ids.shape[1]), F32),
        compiler_params=params(PREPARE_MIB),
        cost_estimate=cost(0, 1 << 18),
    )(ids, weights)


def keep_kernel(tokens_ref, unused_ref, own_ref):
    own_ref[...] = tokens_ref[...]


def keep(tokens, after):
    return pl.pallas_call(
        keep_kernel,
        in_specs=[VMEM, ANY],
        out_shape=jax.ShapeDtypeStruct(tokens.shape, BF16),
        compiler_params=params(PREPARE_MIB),
        cost_estimate=cost(0, 1 << 18),
    )(tokens, after)


def choose_kernel(planes_ref, *refs):
    infos, (chosen_ref, info) = refs[:INFOS], refs[INFOS:]
    gather_info(infos, info, 1)
    unused, hits, here = slot_parts(info[0], planes_ref, chosen_ref.shape[1], infos[0].shape[1])
    chosen_ref[...] = (hits & here).astype(F32).astype(BF16)


def table_kernel(planes_ref, *refs):
    infos, (table_ref, info) = refs[:INFOS], refs[INFOS + 1 :]
    gather_info(infos, info, 3)
    named, unused, here = slot_parts(info[0], planes_ref, table_ref.shape[2], infos[0].shape[1])
    top = len(named)
    for place in range(3):
        value = jnp.zeros(here.shape, F32)
        for k, hit in enumerate(named):
            value = value + jnp.where(hit & here, info[place, :, top + k : top + k + 1], 0.0)
        table_ref[place] = value.astype(BF16)


def from_info(kernel, terms, lead, planes, infos, devices, after=()):
    return pl.pallas_call(
        kernel,
        in_specs=[SMEM] + [VMEM] * INFOS + [ANY] * len(after),
        out_shape=jax.ShapeDtypeStruct((*lead, BLOCKS * STRIDE, devices * BLOCKS * SLOTS), BF16),
        scratch_shapes=[pltpu.VMEM((terms, BLOCKS * STRIDE, infos[0].shape[0]), F32)],
        compiler_params=params(8),
        cost_estimate=cost(1 << 22, 1 << 18),
    )(planes, *infos, *after)


def pick_kernel(chosen_ref, *refs):
    blocks, (out_ref, table) = refs[:BLOCKS], refs[BLOCKS:]
    tokens = blocks[0].shape[0]
    devices, each, features = out_ref.shape
    table[...] = jnp.zeros_like(table)
    for b, block in enumerate(blocks):
        table[b * STRIDE : b * STRIDE + tokens] = block[...]
    for at in range(0, features, CUT):
        cols = slice(at, at + CUT)
        rows = lax.dot_general(
            chosen_ref[...], table[:, cols], (((0,), (0,)), ((), ())), preferred_element_type=F32
        )
        out_ref[:, :, cols] = rows.astype(BF16).reshape(devices, each, CUT)


def pick(chosen, blocks, devices):
    features = blocks[0].shape[1]
    return pl.pallas_call(
        pick_kernel,
        out_shape=jax.ShapeDtypeStruct((devices, BLOCKS * SLOTS, features), BF16),
        scratch_shapes=[pltpu.VMEM((BLOCKS * STRIDE, features), BF16)],
        compiler_params=params(PICK_MIB),
        cost_estimate=cost(1 << 35, 4 << 20),
    )(chosen, *blocks)


def mix_kernel(table_ref, rows_ref, *outs):
    tokens = outs[0].shape[0]
    devices, each, features = rows_ref.shape
    for at in range(0, features, CUT):
        cols = slice(at, at + CUT)
        rows = rows_ref[:, :, cols].reshape(devices * each, CUT)
        total = sum(jnp.dot(table_ref[place], rows, preferred_element_type=F32) for place in range(3))
        for b, out in enumerate(outs):
            out[:, cols] = total[b * STRIDE : b * STRIDE + tokens].astype(out.dtype)


def sum_kernel(own, *refs):
    total = own[...]
    for ref in refs[:-1]:
        total = total + ref[...].astype(F32)
    refs[-1][...] = total.astype(BF16)


def join_kernel(mine_ref, other_ref, out):
    for at in range(0, out.shape[2], CUT):
        parts = [ref[:, :, at : at + CUT].reshape(-1, CUT).astype(F32) for ref in (mine_ref, other_ref)]
        out[:, :, at : at + CUT] = (parts[0] + parts[1]).astype(BF16).reshape(*out.shape[:2], CUT)


def join(mine, other):
    return pl.pallas_call(
        join_kernel,
        out_shape=jax.ShapeDtypeStruct(mine.shape, BF16),
        compiler_params=params(8),
        cost_estimate=cost(1 << 20, 3 << 20),
    )(mine, other)


def expert_kernel(rows_ref, gate, up, down, *refs):
    out_ref, rows, hidden = refs[-3:]
    count, features = rows.shape
    units = hidden.shape[1]
    rows[...] = rows_ref[...].reshape(count, features)
    for at in range(0, units, 256):
        cols = slice(at, at + 256)
        gate_act = jnp.dot(rows[...], gate[:, cols], preferred_element_type=F32)
        up_act = jnp.dot(rows[...], up[:, cols], preferred_element_type=F32)
        hidden[:, cols] = (gate_act / (1.0 + jnp.exp(-gate_act)) * up_act).astype(BF16)
    for at in range(0, features, 256):
        cols = slice(at, at + 256)
        part = jnp.dot(hidden[...], down[:, cols], preferred_element_type=F32).astype(BF16)
        out_ref[:, :, cols] = part.reshape(*out_ref.shape[:2], 256)


def run_expert(rows, gate, up, down, after=()):
    features, units = gate.shape
    count = rows.size // features
    return pl.pallas_call(
        expert_kernel,
        in_specs=[VMEM] * 4 + [ANY] * len(after),
        out_specs=VMEM,
        out_shape=jax.ShapeDtypeStruct(rows.shape, BF16),
        scratch_shapes=[pltpu.VMEM((count, features), BF16), pltpu.VMEM((count, units), BF16)],
        compiler_params=params(FFN_MIB),
        cost_estimate=pl.CostEstimate(
            flops=6 * count * features * units, bytes_accessed=15 << 20, transcendentals=count * units
        ),
    )(rows, gate, up, down, *after)


def on_device(tokens, expert_ids, route_weights, w_gate, w_up, w_down):
    ring, depth, width = lax.axis_size("z"), lax.axis_size("x"), lax.axis_size("y")
    matrices = w_gate[0, 0], w_up[0, 0], w_down[0, 0]
    core, z = lax.axis_index("core"), lax.axis_index("z")
    pair = (z - core + ring) % ring // 2
    planes = jnp.stack([(2 * pair + member + core) % ring for member in range(2)]).astype(jnp.int32)

    def route(by, back):
        pairs = []
        for c in range(2):
            for s in range(ring):
                t = s + by if (s + by) % 2 == 0 else s - by
                pairs.append((c * ring + (s + c) % ring, c * ring + (t + c) % ring))
        return [(b, a) for a, b in pairs] if back else pairs

    def send(value, by, back=False):
        return lax.ppermute(value, ("core", "z"), route(by, back))

    groups = [
        [
            ((y * 2 + c) * depth + x) * ring + (2 * p + member + c) % ring
            for x in range(depth)
            for y in range(width)
            for member in range(2)
        ]
        for c in range(2)
        for p in range(ring // 2)
    ]

    def spread(value):
        return lax.all_to_all(value, AXES, 0, 0, axis_index_groups=groups, tiled=True)

    def swap(value):
        return lax.ppermute(value, "core", [(0, 1), (1, 0)])

    info = prepare(expert_ids.T, route_weights.T)
    own = keep(tokens, info)
    blocks, infos = [tokens], [info]
    blocks += [send(tokens, 1), send(tokens, 2)]
    blocks += [send(blocks[1], 2)]
    infos += [send(info, 1)]
    infos += [send(jnp.concatenate(infos, axis=0), 2)]
    devices = 2 * depth * width
    chosen = from_info(choose_kernel, 1, (), planes, infos, devices)
    mine = spread(pick(chosen, [own] + blocks[1:], devices))
    peer = swap(mine)
    table = from_info(table_kernel, 3, (3,), planes, infos, devices, [mine])
    mine_part = run_expert(mine, *matrices)
    peer_part = run_expert(peer, *matrices, [table])
    returned = spread(join(mine_part, swap(peer_part)))
    shape = tokens.shape
    own, next1, next2, next3 = pl.pallas_call(
        mix_kernel,
        out_shape=[jax.ShapeDtypeStruct(shape, t) for t in (F32, F32, BF16, BF16)],
        compiler_params=params(8),
        cost_estimate=cost(1 << 29, 4 << 20),
    )(table, returned)

    def add(*parts):
        return pl.pallas_call(
            sum_kernel, out_shape=jax.ShapeDtypeStruct(shape, BF16), compiler_params=params(8)
        )(*parts)

    next2, next3 = send(next2, 2, True), send(next3, 2, True)
    return add(own, next2, send(add(next1, next3), 1, True))


def solution(mesh):
    groups, members = mesh.devices.shape
    fine = Mesh(mesh.devices.reshape(groups // 2, 2, 4, members // 4), AXES)
    rows = P(AXES, None)
    weights = P(("y", "core"), ("x", "z"), None, None)
    return jax.shard_map(
        on_device, mesh=fine, in_specs=(rows, rows, rows, weights, weights, weights), out_specs=rows, check_vma=False
    )
```
